256 devices in a mesh: row: 16 (over x, y), col: 16 (over z, core).
Axes of the slice: x: 4, y: 4, z: 8, core: 2. Of those that a mesh axis runs over, the one named last changes fastest.
Arguments:
- inputs: bfloat16 [2048, 6144], P('col', 'row'), may hold values from -6 to 6
- weight: bfloat16 [6144, 24576], P('row', 'col'), may hold values from -0.078125 to 0.078125
- out_grad: bfloat16 [2048, 24576], P('row', 'col'), may hold values from -6 to 6
Outputs:
- activated: bfloat16 [2048, 24576], P('row', 'col')
- input_grad: bfloat16 [2048, 6144], P('col', 'row')
- weight_grad: bfloat16 [6144, 24576], P('row', 'col')
The draws below stay inside these ranges and needn't reach their ends.
All inputs are finite; a program needn't handle non-finite values.
Results may differ from the reference program's by a relative error of at most 0.0049.
Values may be sent and summed in bfloat16 or wider, within the bound.
No kernel may reach another device: no remote copies, remote signals or barrier semaphores. Data moves between devices by JAX's collectives and lax.ppermute only.
A program may use at most 64 MiB of HBM per device.

```python
import jax
import jax.numpy as jnp

D = 6144
H = 24576
TOKENS = 2048


def shard_levels(key, shape, shards, smallest, largest):
    loudness, own = 1.0, jax.random.fold_in(key, 6)
    for axis_at, blocks in shards:
        heights = jnp.exp(jax.random.uniform(jax.random.fold_in(own, axis_at), (blocks,), jnp.float32, smallest / len(shards), largest / len(shards)))
        loudness = loudness * jnp.repeat(heights, shape[axis_at] // blocks).reshape([-1 if axis == axis_at else 1 for axis in range(len(shape))])
    return loudness


def scatter_about(rng, extent, scale, reach, split=(), dtype=jnp.bfloat16):
    values = scale * jax.random.normal(rng, extent, jnp.float32)
    if split:
        values = values * shard_levels(rng, extent, split, -0.22, 0.18)
    return jnp.clip(values, -reach, reach).astype(dtype)


def setup_inputs(seed: int = 0) -> dict:
    key_list = jax.random.split(jax.random.key(seed), 4)
    return {
        "inputs": scatter_about(key_list[0], (TOKENS, D), 1.0, 6.0, ((0, 16), (1, 16))),
        "weight": scatter_about(key_list[1], (D, H), D ** -0.5, 0.078125, ((0, 16), (1, 16))),
        "out_grad": scatter_about(key_list[2], (TOKENS, H), 1.0, 6.0, ((0, 16), (1, 16))),
    }


def activate(value):
    return jax.nn.gelu(value, approximate=True)

def reference(inputs, weight, out_grad):
    preact = jnp.dot(inputs, weight, preferred_element_type=jnp.float32)
    activated, pullback = jax.vjp(activate, preact)
    pre_grad = pullback(out_grad.astype(jnp.float32))[0].astype(jnp.bfloat16)
    input_grad = jnp.dot(pre_grad, weight.T, preferred_element_type=jnp.float32).astype(jnp.bfloat16)
    weight_grad = jnp.dot(inputs.T, pre_grad, preferred_element_type=jnp.float32).astype(jnp.bfloat16)
    return (activated.astype(jnp.bfloat16), input_grad, weight_grad)
```

```python
import jax
import jax.numpy as jnp
from jax import lax
from jax.sharding import PartitionSpec as P

NX, NY, NZ, NC = 4, 4, 8, 2
BOTH = ("row", "col")
STREAMS = (("x", "y"), ("y", "x"))


def activate(value):
    return jax.nn.gelu(value, approximate=True)


def pairs(step):
    out = []
    for x in range(NX):
        for y in range(NY):
            for z in range(NZ):
                for c in range(NC):
                    tx, ty, tz, tc = step(x, y, z, c)
                    source = ((x * NY + y) * NZ + z) * NC + c
                    target = (((tx % NX) * NY + ty % NY) * NZ + tz % NZ) * NC + tc % NC
                    out.append((source, target))
    return out


def way(c):
    return 1 - 2 * c


RING = {
    "x": pairs(lambda x, y, z, c: (x + way(c), y, z, c)),
    "y": pairs(lambda x, y, z, c: (x, y + way(c), z, c)),
    "z": pairs(lambda x, y, z, c: (x, y, z + way(c), c)),
    "core": pairs(lambda x, y, z, c: (x, y, z, 1 - c)),
}


def send(value, ring):
    return lax.ppermute(value, BOTH, RING[ring])


def pick(array, index, axis):
    return lax.dynamic_index_in_dim(array, index, axis, keepdims=False)


def put(array, value, index, axis):
    return lax.dynamic_update_index_in_dim(array, value, index, axis)


def body(inputs, weight, out_grad):
    bf16, f32 = jnp.bfloat16, jnp.float32
    row, col = lax.axis_index("row"), lax.axis_index("col")
    at = {"x": row // NY, "y": row % NY}
    z, core = col // NC, col % NC
    up = way(core)
    tokens, features = inputs.shape
    hidden = weight.shape[1]
    width = hidden // len(STREAMS)

    def near(axis, k):
        return (at[axis] - k * up) % 4

    with jax.named_scope("gather_inputs"):
        other = send(inputs, "core")
        pair = jnp.where(core == 0, jnp.stack([inputs, other]), jnp.stack([other, inputs]))
        whole = jnp.zeros((NZ, NC, tokens, features), bf16)
        whole = put(whole, pair, z, 0)
        block = pair
        for k in range(1, 4):
            block = send(block, "z")
            whole = put(whole, block, (z - k * up) % NZ, 0)
            whole = put(whole, send(block, "core"), (z + k * up) % NZ, 0)
        half = send(pick(block, core, 0), "z")
        rest = send(half, "core")
        far = jnp.where(core == 0, jnp.stack([half, rest]), jnp.stack([rest, half]))
        whole = put(whole, far, (z + 4) % NZ, 0)
        whole = whole.reshape(NX, NY, tokens, features)

    def chunk_of(axis, index):
        taken = pick(whole, index, 0 if axis == "x" else 1)
        return taken.reshape(4 * tokens, features)

    activated, grads = [], []
    for s, (first, second) in enumerate(STREAMS):
        cols = slice(s * width, (s + 1) * width)
        part = weight[:, cols]
        with jax.named_scope("reduce_preact"):
            carry = None
            for k in range(1, 5):
                term = jnp.dot(chunk_of(first, near(first, k)), part, preferred_element_type=f32)
                total = term if carry is None else term + carry.astype(f32)
                if k < 4:
                    carry = send(total.astype(bf16), first)
            total = total.reshape(4, tokens, width)
            carry = None
            for k in range(1, 5):
                term = pick(total, near(second, k), 0)
                preact = term if carry is None else term + carry.astype(f32)
                if k < 4:
                    carry = send(preact.astype(bf16), second)
        with jax.named_scope("gelu"):
            act, pullback = jax.vjp(activate, preact)
            activated.append(act.astype(bf16))
            grads.append(pullback(out_grad[:, cols].astype(f32))[0].astype(bf16))

    partial_in, weight_grad = [], []
    for s, (first, second) in enumerate(STREAMS):
        cols = slice(s * width, (s + 1) * width)
        part = weight[:, cols]
        with jax.named_scope("gather_grad"):
            block = grads[s]
            wide = jnp.zeros((4, tokens, width), bf16)
            wide = put(wide, block, near(second, 0), 0)
            for k in range(1, 4):
                block = send(block, second)
                wide = put(wide, block, near(second, k), 0)
            block = wide.reshape(4 * tokens, width)
            axis = 0 if first == "x" else 1
            sums = jnp.zeros((NX, NY, tokens, features), f32)
            wsum = None
            for k in range(4):
                index = near(first, k)
                following = send(block, first) if k < 3 else None
                term = lax.dot_general(block, part, (((1,), (1,)), ((), ())), preferred_element_type=f32)
                sums = put(sums, term.reshape(4, tokens, features), index, axis)
                term = lax.dot_general(
                    chunk_of(first, index), block, (((0,), (0,)), ((), ())), preferred_element_type=f32
                )
                wsum = term if wsum is None else wsum + term
                block = following
            partial_in.append(sums)
            weight_grad.append(wsum.astype(bf16))

    with jax.named_scope("reduce_input_grad"):
        total = sum(partial_in).reshape(NZ, NC, tokens, features)

        def dest(k):
            return pick(total, (z + k * up) % NZ, 0)

        def away(k):
            return pick(total, (z - k * up) % NZ, 0)

        mine, yours = [], []
        for k in (4, 0):
            block = dest(k)
            mine.append(pick(block, core, 0)[None])
            yours.append(pick(block, 1 - core, 0)[None])
        for k in (3, 2, 1):
            mine.append(dest(k))
            yours.append(away(k))
        got = send(jnp.concatenate(yours), "core")
        kept = jnp.concatenate(mine) + got
        carry = send(kept[0].astype(bf16), "z")
        block = kept[2:4]
        block = put(block, pick(block, core, 0) + carry.astype(f32), core, 0)
        for k in (2, 1):
            carry = send(block.astype(bf16), "z")
            block = kept[8 - 2 * k : 10 - 2 * k] + carry.astype(f32)
        carry = send(block.astype(bf16), "z").astype(f32)
        rest = send(pick(carry, 1 - core, 0), "core")
        input_grad = kept[1] + pick(carry, core, 0) + rest
    return (
        jnp.concatenate(activated, axis=1),
        input_grad.astype(bf16),
        jnp.concatenate(weight_grad, axis=1),
    )


def solution(mesh):
    in_specs = (P("col", "row"), P("row", "col"), P("row", "col"))
    out_specs = (P("row", "col"), P("col", "row"), P("row", "col"))
    return jax.shard_map(body, mesh=mesh, in_specs=in_specs, out_specs=out_specs, check_vma=False)
```

```python
import jax
import jax.numpy as jnp
from jax import lax
from jax.sharding import PartitionSpec as P

NX, NY, NZ, NC = 4, 4, 8, 2
BOTH = ("row", "col")
STREAMS = ("x", "y")


def activate(value):
    return jax.nn.gelu(value, approximate=True)


def pairs(step):
    out = []
    for x in range(NX):
        for y in range(NY):
            for z in range(NZ):
                for c in range(NC):
                    tx, ty, tz, tc = step(x, y, z, c)
                    source = ((x * NY + y) * NZ + z) * NC + c
                    target = (((tx % NX) * NY + ty % NY) * NZ + tz % NZ) * NC + tc % NC
                    out.append((source, target))
    return out


def way(c):
    return 1 - 2 * c


MOVES = {
    "x": lambda d: pairs(lambda x, y, z, c: (x + d * way(c), y, z, c)),
    "y": lambda d: pairs(lambda x, y, z, c: (x, y + d * way(c), z, c)),
    "z": lambda d: pairs(lambda x, y, z, c: (x, y, z + d * way(c), c)),
}
SWAP = pairs(lambda x, y, z, c: (x, y, z, 1 - c))


def send(value, axis, ahead):
    return lax.ppermute(value, BOTH, MOVES[axis](ahead))


def swap(value):
    return lax.ppermute(value, BOTH, SWAP)


def reduce4(term, axis):
    bf16, f32 = jnp.bfloat16, jnp.float32
    far = send(term(2).astype(bf16), axis, 1)
    behind = send(term(3).astype(bf16), axis, -1)
    ahead = send((term(1) + far.astype(f32)).astype(bf16), axis, 1)
    return term(0) + behind.astype(f32) + ahead.astype(f32)


def gather4(block, axis):
    one_behind = send(block, axis, 1)
    one_ahead = send(block, axis, -1)
    far = send(one_behind, axis, 1)
    return [block, one_ahead, far, one_behind]


def body(inputs, weight, out_grad):
    bf16, f32 = jnp.bfloat16, jnp.float32
    row, col = lax.axis_index("row"), lax.axis_index("col")
    x, y = row >> 2, row & 3
    z, core = col >> 1, col & 1
    up = way(core)
    tokens, features = inputs.shape
    hidden = weight.shape[1]
    width = hidden // len(STREAMS)

    def place(dz, other):
        at_z = (z + dz * up) & 7
        at_core = (core + other) & 1
        ahead_x = (((at_z >> 1) - x) * up) & 3
        ahead_y = (((at_z & 1) * 2 + at_core - y) * up) & 3
        return ahead_x * 4 + ahead_y

    with jax.named_scope("gather_inputs"):
        blocks = {(0, 0): inputs, (0, 1): swap(inputs)}
        pair = jnp.stack([blocks[0, 0], blocks[0, 1]])
        one = send(pair, "z", 1)
        two = send(pair, "z", 2)
        three = send(jnp.concatenate([one, two[:1]]), "z", 2)
        near = swap(jnp.concatenate([one, two]))
        rest = swap(three)
        for other in (0, 1):
            blocks[-1, other] = one[other]
            blocks[-2, other] = two[other]
            blocks[-3, other] = three[other]
            blocks[1, 1 - other] = near[other]
            blocks[2, 1 - other] = near[2 + other]
            blocks[3, 1 - other] = rest[other]
        blocks[4, 0] = three[2]
        blocks[4, 1] = rest[2]
        whole = jnp.zeros((16, tokens, features), bf16)
        for (dz, other), block in blocks.items():
            whole = lax.dynamic_update_index_in_dim(whole, block, place(dz, other), 0)
        whole = whole.reshape(4, 4, tokens, features)

    def chunk(axis, ahead):
        taken = whole[ahead] if axis == "x" else whole[:, ahead]
        return taken.reshape(4 * tokens, features)

    activated, grads, parts = [], [], []
    for s, first in enumerate(STREAMS):
        second = STREAMS[1 - s]
        cols = slice(s * width, (s + 1) * width)
        part = weight[:, cols]
        with jax.named_scope("reduce_preact"):
            total = reduce4(
                lambda m: jnp.dot(chunk(first, m), part, preferred_element_type=f32), first
            ).reshape(4, tokens, width)
            preact = reduce4(lambda m: total[m], second)
        with jax.named_scope("gelu"):
            act, pullback = jax.vjp(activate, preact)
            activated.append(act.astype(bf16))
            grads.append(pullback(out_grad[:, cols].astype(f32))[0].astype(bf16))
        parts.append(part)

    partial_in, weight_grad = [], []
    for s, first in enumerate(STREAMS):
        second = STREAMS[1 - s]
        with jax.named_scope("gather_grad"):
            wide = jnp.concatenate(gather4(grads[s], second))
            got = gather4(wide, first)
            sums, wsum = [], None
            for m in (0, 3, 1, 2):
                term = lax.dot_general(
                    got[m], parts[s], (((1,), (1,)), ((), ())), preferred_element_type=f32
                )
                sums.append((m, term.reshape(4, tokens, features)))
                term = lax.dot_general(
                    chunk(first, m), got[m], (((0,), (0,)), ((), ())), preferred_element_type=f32
                )
                wsum = term if wsum is None else wsum + term
            partial_in.append(jnp.stack([dict(sums)[m] for m in range(4)], axis=s))
            weight_grad.append(wsum.astype(bf16))

    with jax.named_scope("reduce_input_grad"):
        total = sum(partial_in).reshape(16, tokens, features)

        def pick(dz, other):
            return lax.dynamic_index_in_dim(total, place(dz, other), 0, keepdims=False)

        order = [(4, 0), (0, 0), (3, 0), (3, 1), (2, 0), (2, 1), (1, 0), (1, 1)]
        mine = jnp.stack([pick(dz, other) for dz, other in order])
        yours = jnp.stack([pick(-dz, 1 - other) for dz, other in order])
        kept = mine + swap(yours)
        late = send(jnp.concatenate([kept[2:4], kept[:1]]).astype(bf16), "z", 2).astype(f32)
        two = send(jnp.stack([kept[4] + late[2], kept[5]]).astype(bf16), "z", 2)
        one = send((kept[6:8] + late[:2]).astype(bf16), "z", 1)
        here = one.astype(f32) + two.astype(f32)
        input_grad = kept[1] + here[0] + swap(here[1])
    return (
        jnp.concatenate(activated, axis=1),
        input_grad.astype(bf16),
        jnp.concatenate(weight_grad, axis=1),
    )


def solution(mesh):
    in_specs = (P("col", "row"), P("row", "col"), P("row", "col"))
    out_specs = (P("row", "col"), P("col", "row"), P("row", "col"))
    return jax.shard_map(body, mesh=mesh, in_specs=in_specs, out_specs=out_specs, check_vma=False)
```

```python
import jax
import jax.numpy as jnp
from jax import lax
from jax.sharding import PartitionSpec as P

NX, NY, NZ, NC = 4, 4, 8, 2
BOTH = ("row", "col")
STREAMS = ("x", "y")


def activate(value):
    return jax.nn.gelu(value, approximate=True)


def pairs(step):
    out = []
    for x in range(NX):
        for y in range(NY):
            for z in range(NZ):
                for c in range(NC):
                    tx, ty, tz, tc = step(x, y, z, c)
                    source = ((x * NY + y) * NZ + z) * NC + c
                    target = (((tx % NX) * NY + ty % NY) * NZ + tz % NZ) * NC + tc % NC
                    out.append((source, target))
    return out


def way(c):
    return 1 - 2 * c


MOVES = {
    "x": lambda d: pairs(lambda x, y, z, c: (x + d * way(c), y, z, c)),
    "y": lambda d: pairs(lambda x, y, z, c: (x, y + d * way(c), z, c)),
    "z": lambda d: pairs(lambda x, y, z, c: (x, y, z + d * way(c), c)),
}
SWAP = pairs(lambda x, y, z, c: (x, y, z, 1 - c))


def send(value, axis, ahead):
    return lax.ppermute(value, BOTH, MOVES[axis](ahead))


def swap(value):
    return lax.ppermute(value, BOTH, SWAP)


def together(*values):
    return lax.optimization_barrier(values)


def reduce4(terms, axes):
    bf16, f32 = jnp.bfloat16, jnp.float32
    out = together(*[term(m).astype(bf16) for m in (2, 3) for term in terms])
    n = len(terms)
    got = [send(out[s], axes[s], 1) for s in range(n)] + [send(out[n + s], axes[s], -1) for s in range(n)]
    got = together(*got, *[term(m) for m in (1, 0) for term in terms])
    far, behind, following, own = got[:n], got[n : 2 * n], got[2 * n : 3 * n], got[3 * n :]
    ahead = [send((following[s] + far[s].astype(f32)).astype(bf16), axes[s], 1) for s in range(n)]
    return [own[s] + behind[s].astype(f32) + ahead[s].astype(f32) for s in range(n)]


def gather4(blocks, axes, work=None):
    n = len(blocks)
    work = work or (lambda s, m, block: ())
    first = [send(blocks[s], axes[s], 1) for s in range(n)] + [send(blocks[s], axes[s], -1) for s in range(n)]
    got, done = together(first, [{0: work(s, 0, blocks[s])} for s in range(n)])
    far = [send(got[s], axes[s], 1) for s in range(n)]
    for s in range(n):
        done[s].update({3: work(s, 3, got[s]), 1: work(s, 1, got[n + s])})
    far, done = together(far, done)
    return [(blocks[s], got[n + s], far[s], got[s]) for s in range(n)], done


def body(inputs, weight, out_grad):
    bf16, f32 = jnp.bfloat16, jnp.float32
    row, col = lax.axis_index("row"), lax.axis_index("col")
    x, y = row >> 2, row & 3
    z, core = col >> 1, col & 1
    up = way(core)
    tokens, features = inputs.shape
    hidden = weight.shape[1]
    width = hidden // len(STREAMS)

    def place(dz, other):
        at_z = (z + dz * up) & 7
        at_core = (core + other) & 1
        ahead_x = (((at_z >> 1) - x) * up) & 3
        ahead_y = (((at_z & 1) * 2 + at_core - y) * up) & 3
        return ahead_x * 4 + ahead_y

    with jax.named_scope("gather_inputs"):
        blocks = {(0, 0): inputs, (0, 1): swap(inputs)}
        pair = jnp.stack([blocks[0, 0], blocks[0, 1]])
        one = send(pair, "z", 1)
        two = send(pair, "z", 2)
        one, two = together(one, two)
        three = send(two, "z", 1)
        four = send(two[0], "z", 2)
        near = swap(jnp.concatenate([one, two]))
        three, four, near = together(three, four, near)
        rest = swap(jnp.concatenate([three, four[None]]))
        for other in (0, 1):
            blocks[-1, other] = one[other]
            blocks[-2, other] = two[other]
            blocks[-3, other] = three[other]
            blocks[1, 1 - other] = near[other]
            blocks[2, 1 - other] = near[2 + other]
            blocks[3, 1 - other] = rest[other]
        blocks[4, 0] = four
        blocks[4, 1] = rest[2]
        whole = jnp.zeros((16, tokens, features), bf16)
        for (dz, other), block in blocks.items():
            whole = lax.dynamic_update_index_in_dim(whole, block, place(dz, other), 0)
        whole = whole.reshape(4, 4, tokens, features)

    def chunk(axis, ahead):
        taken = whole[ahead] if axis == "x" else whole[:, ahead]
        return taken.reshape(4 * tokens, features)

    half = [slice(s * width, (s + 1) * width) for s in range(len(STREAMS))]
    parts = [weight[:, cols] for cols in half]
    crossed = STREAMS[::-1]

    with jax.named_scope("reduce_preact"):
        totals = reduce4(
            [
                lambda m, s=s: jnp.dot(chunk(STREAMS[s], m), parts[s], preferred_element_type=f32)
                for s in range(len(STREAMS))
            ],
            STREAMS,
        )
        totals = [total.reshape(4, tokens, width) for total in totals]
        preacts = reduce4([lambda m, total=total: total[m] for total in totals], crossed)
    activated, grads = [], []
    with jax.named_scope("gelu"):
        for s, cols in enumerate(half):
            act, pullback = jax.vjp(activate, preacts[s])
            activated.append(act.astype(bf16))
            grads.append(pullback(out_grad[:, cols].astype(f32))[0].astype(bf16))

    def to_inputs(s, block):
        term = lax.dot_general(block, parts[s], (((1,), (1,)), ((), ())), preferred_element_type=f32)
        return term.reshape(4, tokens, features)

    def to_weight(s, m, block):
        return lax.dot_general(
            chunk(STREAMS[s], m), block, (((0,), (0,)), ((), ())), preferred_element_type=f32
        )

    with jax.named_scope("gather_grad"):
        got, _ = gather4(grads, crossed)
        wide = []
        for blocks in got:
            whole_block = jnp.zeros((4, tokens, width), bf16)
            for m in range(4):
                whole_block = whole_block.at[m].set(blocks[m])
            wide.append(whole_block.reshape(4 * tokens, width))
        got, done = gather4(
            wide, STREAMS, lambda s, m, block: (to_inputs(s, block), to_weight(s, m, block))
        )
        partial_in = []
        for s in range(len(STREAMS)):
            terms = [done[s][m][0] if m != 2 else to_inputs(s, got[s][2]) for m in range(4)]
            partial_in.append(jnp.stack(terms, axis=s))

    with jax.named_scope("reduce_input_grad"):
        total = sum(partial_in).reshape(16, tokens, features)

        def pick(dz, other):
            return lax.dynamic_index_in_dim(total, place(dz, other), 0, keepdims=False)

        order = [(4, 0), (0, 0), (3, 0), (3, 1), (2, 0), (2, 1), (1, 0), (1, 1)]
        mine = jnp.stack([pick(dz, other) for dz, other in order])
        yours = jnp.stack([pick(-dz, 1 - other) for dz, other in order])
        kept, last = together(mine + swap(yours), [got[s][2] for s in range(len(STREAMS))])
        one = send(kept[6:8].astype(bf16), "z", 1)
        three = send(kept[2:4].astype(bf16), "z", 1)
        four = send(kept[0].astype(bf16), "z", 2)
        weight_grad = [
            (done[s][0][1] + done[s][1][1] + done[s][3][1] + to_weight(s, 2, last[s])).astype(bf16)
            for s in range(len(STREAMS))
        ]
        one, three, four = together(one, three, four)
        two = kept[4:6] + three.astype(f32)
        two = two.at[0].add(four.astype(f32)).astype(bf16)
        here = send(two, "z", 2).astype(f32) + one.astype(f32)
        input_grad = kept[1] + here[0] + swap(here[1])
    return (
        jnp.concatenate(activated, axis=1),
        input_grad.astype(bf16),
        jnp.concatenate(weight_grad, axis=1),
    )


def solution(mesh):
    in_specs = (P("col", "row"), P("row", "col"), P("row", "col"))
    out_specs = (P("row", "col"), P("col", "row"), P("row", "col"))
    return jax.shard_map(body, mesh=mesh, in_specs=in_specs, out_specs=out_specs, check_vma=False)
```

```python
import jax
import jax.numpy as jnp
from jax import lax
from jax.experimental.layout import Layout, with_layout_constraint
from jax.sharding import PartitionSpec as P

NX, NY, NZ, NC = 4, 4, 8, 2
BOTH = ("row", "col")
STREAMS = ("x", "y")


def activate(value):
    return jax.nn.gelu(value, approximate=True)


def pairs(step):
    out = []
    for x in range(NX):
        for y in range(NY):
            for z in range(NZ):
                for c in range(NC):
                    tx, ty, tz, tc = step(x, y, z, c)
                    source = ((x * NY + y) * NZ + z) * NC + c
                    target = (((tx % NX) * NY + ty % NY) * NZ + tz % NZ) * NC + tc % NC
                    out.append((source, target))
    return out


def way(c):
    return 1 - 2 * c


MOVES = {
    "x": lambda d: pairs(lambda x, y, z, c: (x + d * way(c), y, z, c)),
    "y": lambda d: pairs(lambda x, y, z, c: (x, y + d * way(c), z, c)),
    "z": lambda d: pairs(lambda x, y, z, c: (x, y, z + d * way(c), c)),
}
SWAP = pairs(lambda x, y, z, c: (x, y, z, 1 - c))


def send(value, axis, ahead):
    return lax.ppermute(value, BOTH, MOVES[axis](ahead))


def swap(value):
    return lax.ppermute(value, BOTH, SWAP)


def together(*values):
    return lax.optimization_barrier(values)


def plainly(value):
    return with_layout_constraint(value, Layout(major_to_minor=tuple(range(value.ndim))))


def reduce4(terms, axes, *also):
    bf16, f32 = jnp.bfloat16, jnp.float32
    n, order = len(terms), (2, 1, 3)
    out, also = together([plainly(term(m).astype(bf16)) for m in order for term in terms], also)
    got = [send(out[i * n + s], axes[s], order[i]) for i in range(3) for s in range(n)]
    sums = [terms[s](0) + sum(got[i * n + s].astype(f32) for i in range(3)) for s in range(n)]
    return sums, also


def gather4(blocks, axes):
    n = len(blocks)
    blocks = [plainly(block) for block in blocks]
    got = {m: [send(blocks[s], axes[s], -m) for s in range(n)] for m in (2, 1, 3)}
    return [[blocks[s], got[1][s], got[2][s], got[3][s]] for s in range(n)]


def body(inputs, weight, out_grad):
    bf16, f32 = jnp.bfloat16, jnp.float32
    row, col = lax.axis_index("row"), lax.axis_index("col")
    x, y = row >> 2, row & 3
    z, core = col >> 1, col & 1
    up = way(core)
    tokens, features = inputs.shape
    hidden = weight.shape[1]
    width = hidden // 3

    def place(dz, other):
        at_z = (z + dz * up) & 7
        at_core = (core + other) & 1
        ahead_x = (((at_z >> 1) - x) * up) & 3
        ahead_y = (((at_z & 1) * 2 + at_core - y) * up) & 3
        return ahead_x * 4 + ahead_y

    def number(dz, other):
        return ((z + dz * up) & 7) * 2 + ((core + other) & 1)

    with jax.named_scope("gather_inputs"):
        blocks = {(0, 0): inputs, (0, 1): swap(inputs)}
        pair = jnp.stack([blocks[0, 0], blocks[0, 1]])
        one = send(pair, "z", 1)
        two = send(pair, "z", 2)
        one, two = together(one, two)
        three = send(two, "z", 1)
        four = send(two[0], "z", 2)
        near = swap(jnp.concatenate([one, two]))
        three, four, near = together(three, four, near)
        rest = swap(jnp.concatenate([three, four[None]]))
        for other in (0, 1):
            blocks[-1, other] = one[other]
            blocks[-2, other] = two[other]
            blocks[-3, other] = three[other]
            blocks[1, 1 - other] = near[other]
            blocks[2, 1 - other] = near[2 + other]
            blocks[3, 1 - other] = rest[other]
        blocks[4, 0] = four
        blocks[4, 1] = rest[2]
        whole = jnp.zeros((16, tokens, features), bf16)
        plain = jnp.zeros((16, tokens, features), bf16)
        for (dz, other), block in blocks.items():
            whole = lax.dynamic_update_index_in_dim(whole, block, place(dz, other), 0)
            plain = lax.dynamic_update_index_in_dim(plain, block, number(dz, other), 0)
        whole = plainly(whole).reshape(4, 4, tokens, features)
        plain = plainly(plain).reshape(16 * tokens, features)

    def chunk(axis, ahead):
        taken = whole[ahead] if axis == "x" else whole[:, ahead]
        return taken.reshape(4 * tokens, features)

    third = [slice(s * width, (s + 1) * width) for s in range(3)]
    parts = [weight[:, cols] for cols in third]
    streams = range(len(STREAMS))
    crossed = STREAMS[::-1]

    def gelu(preact, cotangent):
        act, pullback = jax.vjp(activate, preact)
        grad = pullback(cotangent.astype(f32))[0]
        return act.astype(bf16), plainly(grad.astype(bf16))

    with jax.named_scope("reduce_preact"):
        beside = jnp.dot(plain, parts[2], preferred_element_type=f32).astype(bf16)
        totals, (beside,) = reduce4(
            [
                lambda m, s=s: jnp.dot(chunk(STREAMS[s], m), parts[s], preferred_element_type=f32)
                for s in streams
            ],
            STREAMS,
            beside,
        )
        beside = lax.psum_scatter(plainly(beside), "row", scatter_dimension=0, tiled=True)
        totals = [total.reshape(4, tokens, width) for total in totals]
        preacts, _ = reduce4([lambda m, total=total: total[m] for total in totals], crossed)
    with jax.named_scope("gelu"):
        activated, grads = zip(*[gelu(preacts[s], out_grad[:, third[s]]) for s in streams])
        grads, cotangent = together(grads, out_grad[:, third[2]])
        act, grad = gelu(beside.astype(f32), cotangent)
        activated += (act,)

    def to_inputs(s, block):
        return lax.dot_general(block, parts[s], (((1,), (1,)), ((), ())), preferred_element_type=f32)

    def to_weight(tokens_of, block):
        return lax.dot_general(tokens_of, block, (((0,), (0,)), ((), ())), preferred_element_type=f32)

    with jax.named_scope("gather_grad"):
        beside = plainly(lax.all_gather(grad, "row", axis=0, tiled=True))
        wide = []
        for blocks in gather4(grads, crossed):
            joined = jnp.zeros((4, tokens, width), bf16)
            for m in range(4):
                joined = joined.at[m].set(blocks[m])
            wide.append(joined.reshape(4 * tokens, width))
        wide = [plainly(block) for block in wide]
        got = gather4(wide, STREAMS)
        early = [to_weight(chunk(STREAMS[s], 0), wide[s]) for s in streams]
        last, early = together([got[s][2] for s in streams], early)
        for s in streams:
            got[s][2] = last[s]
        partial_in = [
            jnp.stack([to_inputs(s, block).reshape(4, tokens, features) for block in got[s]], axis=s)
            for s in streams
        ]

    with jax.named_scope("reduce_input_grad"):
        total = sum(partial_in).reshape(16, tokens, features)
        plain_total = to_inputs(2, beside).reshape(16, tokens, features)

        def pick(dz, other):
            one = lax.dynamic_index_in_dim(total, place(dz, other), 0, keepdims=False)
            return one + lax.dynamic_index_in_dim(plain_total, number(dz, other), 0, keepdims=False)

        order = [(4, 0), (0, 0), (3, 0), (3, 1), (2, 0), (2, 1), (1, 0), (1, 1)]
        mine = jnp.stack([pick(dz, other) for dz, other in order])
        yours = jnp.stack([pick(-dz, 1 - other) for dz, other in order])
        kept, got, beside = together(mine + swap(yours), got, beside)
        one = send(kept[6:8].astype(bf16), "z", 1)
        three = send(kept[2:4].astype(bf16), "z", 1)
        four = send(kept[0].astype(bf16), "z", 2)
        weight_grad = [
            sum((to_weight(chunk(STREAMS[s], m), got[s][m]) for m in (1, 2, 3)), early[s]).astype(bf16)
            for s in streams
        ]
        weight_grad.append(to_weight(plain, beside).astype(bf16))
        one, three, four = together(one, three, four)
        two = kept[4:6] + three.astype(f32)
        two = two.at[0].add(four.astype(f32)).astype(bf16)
        here = send(two, "z", 2).astype(f32) + one.astype(f32)
        input_grad = kept[1] + here[0] + swap(here[1])
    return (
        jnp.concatenate(activated, axis=1),
        input_grad.astype(bf16),
        jnp.concatenate(weight_grad, axis=1),
    )


def solution(mesh):
    in_specs = (P("col", "row"), P("row", "col"), P("row", "col"))
    out_specs = (P("row", "col"), P("col", "row"), P("row", "col"))
    return jax.shard_map(body, mesh=mesh, in_specs=in_specs, out_specs=out_specs, check_vma=False)
```

```python
import jax
import jax.numpy as jnp
from jax import lax
from jax.experimental.layout import Layout, with_layout_constraint
from jax.sharding import PartitionSpec as P

NX, NY, NZ, NC = 4, 4, 8, 2
BOTH = ("row", "col")


def activate(value):
    return jax.nn.gelu(value, approximate=True)


def pairs(step):
    out = []
    for x in range(NX):
        for y in range(NY):
            for z in range(NZ):
                for c in range(NC):
                    tx, ty, tz, tc = step(x, y, z, c)
                    source = ((x * NY + y) * NZ + z) * NC + c
                    target = (((tx % NX) * NY + ty % NY) * NZ + tz % NZ) * NC + tc % NC
                    out.append((source, target))
    return out


def way(c):
    return 1 - 2 * c


def along(first):
    return lambda d: pairs(
        lambda x, y, z, c: (x + d, y, z, c) if (c == 0) == first else (x, y + d, z, c)
    )


MOVES = {
    "first": along(True),
    "second": along(False),
    "z": lambda d: pairs(lambda x, y, z, c: (x, y, z + d * way(c), c)),
}
SWAP = pairs(lambda x, y, z, c: (x, y, z, 1 - c))


def send(value, axis, ahead):
    return lax.ppermute(value, BOTH, MOVES[axis](ahead))


def swap(value):
    return lax.ppermute(value, BOTH, SWAP)


def plainly(value):
    return with_layout_constraint(value, Layout(major_to_minor=tuple(range(value.ndim))))


def together(*values):
    return lax.optimization_barrier(values)


def reduce4(above, below, near_above, near_below, own, axis):
    bf16, f32 = jnp.bfloat16, jnp.float32
    half = above.shape[0] // 2
    above, below = together(plainly(above.astype(bf16)), plainly(below.astype(bf16)))
    from_below, from_above = send(above, axis, 1), send(below, axis, -1)
    from_below, from_above, near_above, near_below, own = together(
        from_below, from_above, near_above, near_below, own
    )
    late_below = send((near_above + from_below[half:].astype(f32)).astype(bf16), axis, 1)
    late_above = send((near_below + from_above[:half].astype(f32)).astype(bf16), axis, -1)
    return (
        own[:half] + from_above[half:].astype(f32) + late_below.astype(f32),
        own[half:] + from_below[:half].astype(f32) + late_above.astype(f32),
    )


def gather4(block, axis, work=None, later=None):
    half = block.shape[0] // 2
    block = plainly(block)
    down, up = send(block, axis, 1), send(block, axis, -1)
    down, up, done = together(down, up, work() if work else ())
    far = (send(down[:half], axis, 1), send(up[half:], axis, -1))
    far, rest = together(far, later(up, down) if later else ())
    return up, down, far, done, rest


def body(inputs, weight, out_grad):
    bf16, f32 = jnp.bfloat16, jnp.float32
    row, col = lax.axis_index("row"), lax.axis_index("col")
    x, y = row >> 2, row & 3
    z, core = col >> 1, col & 1
    up = way(core)
    tokens, features = inputs.shape
    hidden = weight.shape[1]

    def place(dz, other):
        at_z = (z + dz * up) & 7
        at_x, at_y = at_z >> 1, (at_z & 1) * 2 + ((core + other) & 1)
        return jnp.where(core == 0, ((at_x - x) & 3) * 4 + at_y, ((at_y - y) & 3) * 4 + at_x)

    with jax.named_scope("gather_inputs"):
        blocks = {(0, 0): inputs, (0, 1): swap(inputs)}
        pair = jnp.stack([blocks[0, 0], blocks[0, 1]])
        one = send(pair, "z", 1)
        two = send(pair, "z", 2)
        one, two = together(one, two)
        three = send(two, "z", 1)
        four = send(two[0], "z", 2)
        near = swap(jnp.concatenate([one, two]))
        three, four, near = together(three, four, near)
        rest = swap(jnp.concatenate([three, four[None]]))
        for other in (0, 1):
            blocks[-1, other] = one[other]
            blocks[-2, other] = two[other]
            blocks[-3, other] = three[other]
            blocks[1, 1 - other] = near[other]
            blocks[2, 1 - other] = near[2 + other]
            blocks[3, 1 - other] = rest[other]
        blocks[4, 0] = four
        blocks[4, 1] = rest[2]
        whole = jnp.zeros((16, tokens, features), bf16)
        for (dz, other), block in blocks.items():
            whole = lax.dynamic_update_index_in_dim(whole, block, place(dz, other), 0)
        whole = plainly(whole)

    def chunk(start, stop):
        return whole[start:stop].reshape((stop - start) * tokens, features)

    with jax.named_scope("reduce_preact"):

        def part(start, stop):
            return jnp.dot(chunk(start, stop), weight, preferred_element_type=f32)

        totals = reduce4(part(6, 10), part(10, 14), part(4, 6), part(14, 16), part(0, 4), "first")
        total = jnp.concatenate(totals).reshape(4, tokens, hidden)
        half = tokens // 2
        second = jnp.where(core == 0, y, x)
        own, above, far, below = [
            lax.dynamic_index_in_dim(total, (second + m) & 3, 0, keepdims=False) for m in range(4)
        ]
        preact = jnp.concatenate(
            reduce4(
                jnp.concatenate([above[half:], far[:half]]),
                jnp.concatenate([far[half:], below[:half]]),
                above[:half],
                below[half:],
                own,
                "second",
            )
        )
    with jax.named_scope("gelu"):
        activated, pullback = jax.vjp(activate, preact)
        grad = pullback(out_grad.astype(f32))[0].astype(bf16)

    def to_inputs(block):
        return lax.dot_general(block, weight, (((1,), (1,)), ((), ())), preferred_element_type=f32)

    def to_weight(start, stop, block):
        return lax.dot_general(
            chunk(start, stop), block, (((0,), (0,)), ((), ())), preferred_element_type=f32
        )

    with jax.named_scope("gather_grad"):
        above, below, far, _, _ = gather4(grad, "second")
        wide = jnp.zeros((4, tokens, hidden), bf16)
        for m, block in enumerate((grad, above, far, below)):
            place_m = (second + m) & 3
            if m == 2:
                for h in range(2):
                    wide = lax.dynamic_update_slice(wide, block[h][None], (place_m, h * half, 0))
            else:
                wide = lax.dynamic_update_index_in_dim(wide, block, place_m, 0)
        wide = plainly(wide.reshape(4 * tokens, hidden))
        above, below, far, (in_own, w_own), (in_above, in_below, w_sum) = gather4(
            wide,
            "first",
            lambda: (to_inputs(wide), to_weight(0, 4, wide)),
            lambda up, down: (
                to_inputs(up),
                to_inputs(down),
                to_weight(4, 8, up) + to_weight(12, 16, down),
            ),
        )
        in_far = [to_inputs(block) for block in far]

    with jax.named_scope("reduce_input_grad"):
        total = jnp.concatenate([in_own, in_above, *in_far, in_below]).reshape(16, tokens, features)

        def pick(dz, other):
            return lax.dynamic_index_in_dim(total, place(dz, other), 0, keepdims=False)

        order = [(4, 0), (0, 0), (3, 0), (3, 1), (2, 0), (2, 1), (1, 0), (1, 1)]
        mine = jnp.stack([pick(dz, other) for dz, other in order])
        yours = jnp.stack([pick(-dz, 1 - other) for dz, other in order])
        kept, far = together(mine + swap(yours), far)
        one = send(kept[6:8].astype(bf16), "z", 1)
        three = send(kept[2:4].astype(bf16), "z", 1)
        four = send(kept[0].astype(bf16), "z", 2)
        w_far = to_weight(8, 10, far[0]) + to_weight(10, 12, far[1])
        weight_grad = (w_own + w_sum + w_far).astype(bf16)
        one, three, four = together(one, three, four)
        two = kept[4:6] + three.astype(f32)
        two = two.at[0].add(four.astype(f32)).astype(bf16)
        here = send(two, "z", 2).astype(f32) + one.astype(f32)
        input_grad = kept[1] + here[0] + swap(here[1])
    return activated.astype(bf16), input_grad.astype(bf16), weight_grad


def solution(mesh):
    in_specs = (P("col", "row"), P("row", "col"), P("row", "col"))
    out_specs = (P("row", "col"), P("col", "row"), P("row", "col"))
    return jax.shard_map(body, mesh=mesh, in_specs=in_specs, out_specs=out_specs, check_vma=False)
```

```python
import jax
import jax.numpy as jnp
from jax import lax
from jax.experimental.layout import Layout, with_layout_constraint
from jax.sharding import PartitionSpec as P

NX, NY, NZ, NC = 4, 4, 8, 2
BOTH = ("row", "col")


def activate(value):
    return jax.nn.gelu(value, approximate=True)


def pairs(step):
    out = []
    for x in range(NX):
        for y in range(NY):
            for z in range(NZ):
                for c in range(NC):
                    tx, ty, tz, tc = step(x, y, z, c)
                    source = ((x * NY + y) * NZ + z) * NC + c
                    target = (((tx % NX) * NY + ty % NY) * NZ + tz % NZ) * NC + tc % NC
                    out.append((source, target))
    return out


def way(c):
    return 1 - 2 * c


def along(first):
    return lambda d: pairs(
        lambda x, y, z, c: (x + d, y, z, c) if (c == 0) == first else (x, y + d, z, c)
    )


MOVES = {
    "first": along(True),
    "second": along(False),
    "z": lambda d: pairs(lambda x, y, z, c: (x, y, z + d * way(c), c)),
}
SWAP = pairs(lambda x, y, z, c: (x, y, z, 1 - c))


def send(value, axis, ahead):
    return lax.ppermute(value, BOTH, MOVES[axis](ahead))


def swap(value):
    return lax.ppermute(value, BOTH, SWAP)


def plainly(value):
    return with_layout_constraint(value, Layout(major_to_minor=tuple(range(value.ndim))))


def together(*values):
    return lax.optimization_barrier(values)


def reduce4(term, axis):
    bf16, f32 = jnp.bfloat16, jnp.float32
    out = together(*[plainly(term(m, h).astype(bf16)) for m, h in ((2, 0), (2, 1), (1, 1), (3, 0))])
    far_up, far_down = send(out[0], axis, 1), send(out[1], axis, -1)
    direct = [send(out[3], axis, -1), send(out[2], axis, 1)]
    relayed = [
        send((term(1, 0) + far_up.astype(f32)).astype(bf16), axis, 1),
        send((term(3, 1) + far_down.astype(f32)).astype(bf16), axis, -1),
    ]
    return [term(0, h) + direct[h].astype(f32) + relayed[h].astype(f32) for h in range(2)]


def gather4(halves, axis):
    halves = [plainly(half) for half in halves]
    down = [send(halves[0], axis, 1), None]
    up = [None, send(halves[1], axis, -1)]
    down[1] = send(halves[1], axis, 1)
    up[0] = send(halves[0], axis, -1)
    far = [send(down[0], axis, 1), send(up[1], axis, -1)]
    return [halves, up, far, down]


def body(inputs, weight, out_grad):
    bf16, f32 = jnp.bfloat16, jnp.float32
    row, col = lax.axis_index("row"), lax.axis_index("col")
    x, y = row >> 2, row & 3
    z, core = col >> 1, col & 1
    up = way(core)
    tokens, features = inputs.shape
    hidden = weight.shape[1]

    def place(dz, other):
        at_z = (z + dz * up) & 7
        at_x, at_y = at_z >> 1, (at_z & 1) * 2 + ((core + other) & 1)
        return jnp.where(core == 0, ((at_x - x) & 3) * 4 + at_y, ((at_y - y) & 3) * 4 + at_x)

    with jax.named_scope("gather_inputs"):
        blocks = {(0, 0): inputs, (0, 1): swap(inputs)}
        pair = jnp.stack([blocks[0, 0], blocks[0, 1]])
        one = send(pair, "z", 1)
        two = send(pair, "z", 2)
        one, two = together(one, two)
        three = send(two, "z", 1)
        four = send(two[0], "z", 2)
        one, two, three, four = together(one, two, three, four)
        crossed = [swap(block) for block in (one, two, three, four)]
        for other in (0, 1):
            blocks[-1, other] = one[other]
            blocks[-2, other] = two[other]
            blocks[-3, other] = three[other]
            for dz in (1, 2, 3):
                blocks[dz, 1 - other] = crossed[dz - 1][other]
        blocks[4, 0] = four
        blocks[4, 1] = crossed[3]
        whole = jnp.zeros((16, tokens, features), bf16)
        for (dz, other), block in blocks.items():
            whole = lax.dynamic_update_index_in_dim(whole, block, place(dz, other), 0)
        whole = plainly(whole)

    def chunk(start, stop):
        return whole[start:stop].reshape((stop - start) * tokens, features)

    half = tokens // 2
    second = jnp.where(core == 0, y, x)
    with jax.named_scope("reduce_preact"):

        def part(m, h):
            start = 4 * m + 2 * h
            return jnp.dot(chunk(start, start + 2), weight, preferred_element_type=f32)

        total = jnp.concatenate(reduce4(part, "first")).reshape(4, 2, half, hidden)

        def piece(m, h):
            return lax.dynamic_index_in_dim(total[:, h], (second + m) & 3, 0, keepdims=False)

        preact = jnp.concatenate(reduce4(piece, "second"))
    with jax.named_scope("gelu"):
        activated, pullback = jax.vjp(activate, preact)
        grad = pullback(out_grad.astype(f32))[0].astype(bf16)

    def to_inputs(block):
        return lax.dot_general(block, weight, (((1,), (1,)), ((), ())), preferred_element_type=f32)

    def to_weight(start, stop, block):
        return lax.dot_general(
            chunk(start, stop), block, (((0,), (0,)), ((), ())), preferred_element_type=f32
        )

    with jax.named_scope("gather_grad"):
        wide = jnp.zeros((4, tokens, hidden), bf16)
        for m, blocks in enumerate(gather4([grad[:half], grad[half:]], "second")):
            for h in range(2):
                wide = lax.dynamic_update_slice(wide, blocks[h][None], ((second + m) & 3, h * half, 0))
        got = gather4([wide[:2].reshape(2 * tokens, hidden), wide[2:].reshape(2 * tokens, hidden)], "first")
        total = jnp.concatenate([to_inputs(got[m][h]) for m in range(4) for h in range(2)])

    with jax.named_scope("reduce_input_grad"):
        total = total.reshape(16, tokens, features)

        def pick(dz, other):
            return lax.dynamic_index_in_dim(total, place(dz, other), 0, keepdims=False)

        order = [(4, 0), (0, 0), (3, 0), (3, 1), (2, 0), (2, 1), (1, 0), (1, 1)]
        mine = jnp.stack([pick(dz, other) for dz, other in order])
        yours = jnp.stack([pick(-dz, 1 - other) for dz, other in order])
        kept, got = together(mine + swap(yours.astype(bf16)).astype(f32), got)
        one = send(kept[6:8].astype(bf16), "z", 1)
        three = send(kept[2:4].astype(bf16), "z", 1)
        four = send(kept[0].astype(bf16), "z", 2)
        weight_grad = sum(
            to_weight(4 * m + 2 * h, 4 * m + 2 * h + 2, got[m][h]) for m in range(4) for h in range(2)
        ).astype(bf16)
        one, three, four = together(one, three, four)
        two = kept[4:6] + three.astype(f32)
        two = two.at[0].add(four.astype(f32)).astype(bf16)
        here = send(two, "z", 2).astype(f32) + one.astype(f32)
        input_grad = kept[1] + here[0] + swap(here[1])
    return activated.astype(bf16), input_grad.astype(bf16), weight_grad


def solution(mesh):
    in_specs = (P("col", "row"), P("row", "col"), P("row", "col"))
    out_specs = (P("row", "col"), P("col", "row"), P("row", "col"))
    return jax.shard_map(body, mesh=mesh, in_specs=in_specs, out_specs=out_specs, check_vma=False)
```

```python
import jax
import jax.numpy as jnp
from jax import lax
from jax.experimental.layout import Layout, with_layout_constraint
from jax.sharding import PartitionSpec as P

NX, NY, NZ, NC = 4, 4, 8, 2
BOTH = ("row", "col")


def activate(value):
    return jax.nn.gelu(value, approximate=True)


def pairs(step):
    out = []
    for x in range(NX):
        for y in range(NY):
            for z in range(NZ):
                for c in range(NC):
                    tx, ty, tz, tc = step(x, y, z, c)
                    source = ((x * NY + y) * NZ + z) * NC + c
                    target = (((tx % NX) * NY + ty % NY) * NZ + tz % NZ) * NC + tc % NC
                    out.append((source, target))
    return out


def way(c):
    return 1 - 2 * c


def along(first):
    return lambda d: pairs(
        lambda x, y, z, c: (x + d, y, z, c) if (c == 0) == first else (x, y + d, z, c)
    )


MOVES = {
    "first": along(True),
    "second": along(False),
    "z": lambda d: pairs(lambda x, y, z, c: (x, y, z + d * way(c), c)),
}
SWAP = pairs(lambda x, y, z, c: (x, y, z, 1 - c))


def send(value, axis, ahead):
    return lax.ppermute(value, BOTH, MOVES[axis](ahead))


def swap(value):
    return lax.ppermute(value, BOTH, SWAP)


def plainly(value):
    return with_layout_constraint(value, Layout(major_to_minor=tuple(range(value.ndim))))


def together(*values):
    return lax.optimization_barrier(values)


def reduce4(term, axis):
    bf16, f32 = jnp.bfloat16, jnp.float32
    out = together(*[plainly(term(m, h).astype(bf16)) for m, h in ((2, 0), (2, 1), (1, 1), (3, 0))])
    far_up, far_down = send(out[0], axis, 1), send(out[1], axis, -1)
    direct = [send(out[3], axis, -1), send(out[2], axis, 1)]
    relayed = [
        send((term(1, 0) + far_up.astype(f32)).astype(bf16), axis, 1),
        send((term(3, 1) + far_down.astype(f32)).astype(bf16), axis, -1),
    ]
    return [term(0, h) + direct[h].astype(f32) + relayed[h].astype(f32) for h in range(2)]


def reduce4_direct(term, axis):
    bf16, f32 = jnp.bfloat16, jnp.float32
    out = together(*[plainly(term(m).astype(bf16)) for m in (2, 1, 3)])
    got = [send(part, axis, m) for part, m in zip(out, (2, 1, 3))]
    return sum((part.astype(f32) for part in got), term(0))


def gather4_direct(block, axis):
    block = plainly(block)
    got = {m: send(block, axis, -m) for m in (2, 1, 3)}
    return [block, got[1], got[2], got[3]]


def gather4(halves, axis):
    halves = [plainly(half) for half in halves]
    down = [send(halves[0], axis, 1), None]
    up = [None, send(halves[1], axis, -1)]
    down[1] = send(halves[1], axis, 1)
    up[0] = send(halves[0], axis, -1)
    far = [send(down[0], axis, 1), send(up[1], axis, -1)]
    return [halves, up, far, down]


def body(inputs, weight, out_grad):
    bf16, f32 = jnp.bfloat16, jnp.float32
    row, col = lax.axis_index("row"), lax.axis_index("col")
    x, y = row >> 2, row & 3
    z, core = col >> 1, col & 1
    up = way(core)
    tokens, features = inputs.shape
    hidden = weight.shape[1]

    def place(dz, other):
        at_z = (z + dz * up) & 7
        at_x, at_y = at_z >> 1, (at_z & 1) * 2 + ((core + other) & 1)
        return jnp.where(core == 0, ((at_x - x) & 3) * 4 + at_y, ((at_y - y) & 3) * 4 + at_x)

    with jax.named_scope("gather_inputs"):
        blocks = {(0, 0): inputs, (0, 1): swap(inputs)}
        pair = jnp.stack([blocks[0, 0], blocks[0, 1]])
        one = send(pair, "z", 1)
        two = send(pair, "z", 2)
        one, two = together(one, two)
        three = send(two, "z", 1)
        four = send(two[0], "z", 2)
        one, two, three, four = together(one, two, three, four)
        crossed = [swap(block) for block in (one, two, three, four)]
        for other in (0, 1):
            blocks[-1, other] = one[other]
            blocks[-2, other] = two[other]
            blocks[-3, other] = three[other]
            for dz in (1, 2, 3):
                blocks[dz, 1 - other] = crossed[dz - 1][other]
        blocks[4, 0] = four
        blocks[4, 1] = crossed[3]
        whole = jnp.zeros((16, tokens, features), bf16)
        for (dz, other), block in blocks.items():
            whole = lax.dynamic_update_index_in_dim(whole, block, place(dz, other), 0)
        whole = plainly(whole)

    def chunk(start, stop):
        return whole[start:stop].reshape((stop - start) * tokens, features)

    second = jnp.where(core == 0, y, x)
    with jax.named_scope("reduce_preact"):

        def part(m, h):
            start = 4 * m + 2 * h
            return jnp.dot(chunk(start, start + 2), weight, preferred_element_type=f32)

        total = jnp.concatenate(reduce4(part, "first")).reshape(4, tokens, hidden)

        def piece(m):
            return lax.dynamic_index_in_dim(total, (second + m) & 3, 0, keepdims=False)

        preact = reduce4_direct(piece, "second")
    with jax.named_scope("gelu"):
        activated, pullback = jax.vjp(activate, preact)
        grad = pullback(out_grad.astype(f32))[0].astype(bf16)

    def to_inputs(block):
        return lax.dot_general(block, weight, (((1,), (1,)), ((), ())), preferred_element_type=f32)

    def to_weight(start, stop, block):
        return lax.dot_general(
            chunk(start, stop), block, (((0,), (0,)), ((), ())), preferred_element_type=f32
        )

    with jax.named_scope("gather_grad"):
        wide = jnp.zeros((4, tokens, hidden), bf16)
        for m, block in enumerate(gather4_direct(grad, "second")):
            wide = lax.dynamic_update_index_in_dim(wide, block, (second + m) & 3, 0)
        got = gather4([wide[:2].reshape(2 * tokens, hidden), wide[2:].reshape(2 * tokens, hidden)], "first")
        total = jnp.concatenate([to_inputs(got[m][h]) for m in range(4) for h in range(2)])

    with jax.named_scope("reduce_input_grad"):
        total = total.reshape(16, tokens, features)

        def pick(dz, other):
            return lax.dynamic_index_in_dim(total, place(dz, other), 0, keepdims=False)

        order = [(4, 0), (0, 0), (3, 0), (3, 1), (1, 0), (1, 1), (2, 0), (2, 1)]
        mine = jnp.stack([pick(dz, other) for dz, other in order])
        yours = jnp.stack([pick(-dz, 1 - other) for dz, other in order])
        kept, got = together(mine + swap(yours.astype(bf16)).astype(f32), got)
        near = send(kept[2:6].astype(bf16), "z", 1)
        four = send(kept[0].astype(bf16), "z", 2)
        dots = [to_weight(4 * m + 2 * h, 4 * m + 2 * h + 2, got[m][h]) for m in range(4) for h in range(2)]
        near, four = together(near, four)
        two = kept[6:8] + near[:2].astype(f32)
        two = two.at[0].add(four.astype(f32)).astype(bf16)
        two, weight_grad = together(send(two, "z", 2), sum(dots).astype(bf16))
        here = two.astype(f32) + near[2:].astype(f32)
        input_grad = kept[1] + here[0] + swap(here[1])
    return activated.astype(bf16), input_grad.astype(bf16), weight_grad


def solution(mesh):
    in_specs = (P("col", "row"), P("row", "col"), P("row", "col"))
    out_specs = (P("row", "col"), P("col", "row"), P("row", "col"))
    return jax.shard_map(body, mesh=mesh, in_specs=in_specs, out_specs=out_specs, check_vma=False)
```

```python
import jax
import jax.numpy as jnp
from jax import lax
from jax.experimental.layout import Layout, with_layout_constraint
from jax.sharding import PartitionSpec as P

NX, NY, NZ, NC = 4, 4, 8, 2
BOTH = ("row", "col")


def activate(value):
    return jax.nn.gelu(value, approximate=True)


def pairs(step):
    out = []
    for x in range(NX):
        for y in range(NY):
            for z in range(NZ):
                for c in range(NC):
                    tx, ty, tz, tc = step(x, y, z, c)
                    source = ((x * NY + y) * NZ + z) * NC + c
                    target = (((tx % NX) * NY + ty % NY) * NZ + tz % NZ) * NC + tc % NC
                    out.append((source, target))
    return out


def way(c):
    return 1 - 2 * c


def along(first):
    return lambda d: pairs(
        lambda x, y, z, c: (x + d, y, z, c) if (c == 0) == first else (x, y + d, z, c)
    )


MOVES = {
    "first": along(True),
    "second": along(False),
    "z": lambda d: pairs(lambda x, y, z, c: (x, y, z + d * way(c), c)),
}
SWAP = pairs(lambda x, y, z, c: (x, y, z, 1 - c))


def send(value, axis, ahead):
    return lax.ppermute(value, BOTH, MOVES[axis](ahead))


def swap(value):
    return lax.ppermute(value, BOTH, SWAP)


def plainly(value):
    return with_layout_constraint(value, Layout(major_to_minor=tuple(range(value.ndim))))


def together(*values):
    return lax.optimization_barrier(values)


def reduce4(term, axis):
    bf16, f32 = jnp.bfloat16, jnp.float32
    out = together(*[plainly(term(m, h).astype(bf16)) for m, h in ((2, 0), (2, 1), (1, 1), (3, 0))])
    far_up, far_down = send(out[0], axis, 1), send(out[1], axis, -1)
    direct = [send(out[3], axis, -1), send(out[2], axis, 1)]
    relayed = [
        send((term(1, 0) + far_up.astype(f32)).astype(bf16), axis, 1),
        send((term(3, 1) + far_down.astype(f32)).astype(bf16), axis, -1),
    ]
    sums = [term(0, h) + direct[h].astype(f32) for h in range(2)]
    sums, relayed = together(sums, relayed)
    return [sums[h] + relayed[h].astype(f32) for h in range(2)]


def reduce4_direct(term, axis):
    bf16, f32 = jnp.bfloat16, jnp.float32
    out = together(*[plainly(term(m).astype(bf16)) for m in (2, 1, 3)])
    got = [send(part, axis, m) for part, m in zip(out, (2, 1, 3))]
    return sum((part.astype(f32) for part in got), term(0))


def gather4_direct(block, axis):
    block = plainly(block)
    got = {m: send(block, axis, -m) for m in (2, 1, 3)}
    return [block, got[1], got[2], got[3]]


def gather4(halves, axis):
    halves = [plainly(half) for half in halves]
    down = [send(halves[0], axis, 1), None]
    up = [None, send(halves[1], axis, -1)]
    down[1] = send(halves[1], axis, 1)
    up[0] = send(halves[0], axis, -1)
    far = [send(down[0], axis, 1), send(up[1], axis, -1)]
    return [halves, up, far, down]


def body(inputs, weight, out_grad):
    bf16, f32 = jnp.bfloat16, jnp.float32
    row, col = lax.axis_index("row"), lax.axis_index("col")
    x, y = row >> 2, row & 3
    z, core = col >> 1, col & 1
    up = way(core)
    tokens, features = inputs.shape
    hidden = weight.shape[1]

    def place(dz, other):
        at_z = (z + dz * up) & 7
        at_x, at_y = at_z >> 1, (at_z & 1) * 2 + ((core + other) & 1)
        return jnp.where(core == 0, ((at_x - x) & 3) * 4 + at_y, ((at_y - y) & 3) * 4 + at_x)

    with jax.named_scope("gather_inputs"):
        blocks = {(0, 0): inputs, (0, 1): swap(inputs)}
        pair = jnp.stack([blocks[0, 0], blocks[0, 1]])
        one = send(pair, "z", 1)
        two = send(pair, "z", 2)
        one, two = together(one, two)
        three = send(two, "z", 1)
        four = send(two[0], "z", 2)
        one, two, three, four = together(one, two, three, four)
        crossed = [swap(block) for block in (one, two, three, four)]
        for other in (0, 1):
            blocks[-1, other] = one[other]
            blocks[-2, other] = two[other]
            blocks[-3, other] = three[other]
            for dz in (1, 2, 3):
                blocks[dz, 1 - other] = crossed[dz - 1][other]
        blocks[4, 0] = four
        blocks[4, 1] = crossed[3]
        whole = jnp.zeros((16, tokens, features), bf16)
        for (dz, other), block in blocks.items():
            whole = lax.dynamic_update_index_in_dim(whole, block, place(dz, other), 0)
        whole = plainly(whole)

    def chunk(start, stop):
        return whole[start:stop].reshape((stop - start) * tokens, features)

    second = jnp.where(core == 0, y, x)
    with jax.named_scope("reduce_preact"):

        def part(m, h):
            start = 4 * m + 2 * h
            return jnp.dot(chunk(start, start + 2), weight, preferred_element_type=f32)

        total = jnp.concatenate(reduce4(part, "first")).reshape(4, tokens, hidden)

        def piece(m):
            return lax.dynamic_index_in_dim(total, (second + m) & 3, 0, keepdims=False)

        preact = reduce4_direct(piece, "second")
    with jax.named_scope("gelu"):
        activated, pullback = jax.vjp(activate, preact)
        grad = pullback(out_grad.astype(f32))[0].astype(bf16)

    def to_inputs(block):
        return lax.dot_general(block, weight, (((1,), (1,)), ((), ())), preferred_element_type=f32)

    def to_weight(start, stop, block):
        return lax.dot_general(
            chunk(start, stop), block, (((0,), (0,)), ((), ())), preferred_element_type=f32
        )

    with jax.named_scope("gather_grad"):
        wide = jnp.zeros((4, tokens, hidden), bf16)
        gathered, activated = together(gather4_direct(grad, "second"), activated.astype(bf16))
        for m, block in enumerate(gathered):
            wide = lax.dynamic_update_index_in_dim(wide, block, (second + m) & 3, 0)
        got = gather4([wide[:2].reshape(2 * tokens, hidden), wide[2:].reshape(2 * tokens, hidden)], "first")
        total = jnp.concatenate([to_inputs(got[m][h]) for m in range(4) for h in range(2)])

    with jax.named_scope("reduce_input_grad"):
        total = total.reshape(16, tokens, features)

        def pick(dz, other):
            return lax.dynamic_index_in_dim(total, place(dz, other), 0, keepdims=False)

        order = [(4, 0), (0, 0), (3, 0), (3, 1), (1, 0), (1, 1), (2, 0), (2, 1)]
        mine = jnp.stack([pick(dz, other) for dz, other in order])
        yours = jnp.stack([pick(-dz, 1 - other) for dz, other in order])
        kept, got = together(mine + swap(yours.astype(bf16)).astype(f32), got)
        near = send(kept[2:6].astype(bf16), "z", 1)
        four = send(kept[0].astype(bf16), "z", 2)
        dots = [to_weight(4 * m + 2 * h, 4 * m + 2 * h + 2, got[m][h]) for m in range(4) for h in range(2)]
        near, four = together(near, four)
        two = kept[6:8] + near[:2].astype(f32)
        two = two.at[0].add(four.astype(f32)).astype(bf16)
        two, weight_grad = together(send(two, "z", 2), sum(dots).astype(bf16))
        here = two.astype(f32) + near[2:].astype(f32)
        input_grad = kept[1] + here[0] + swap(here[1])
    return activated, input_grad.astype(bf16), weight_grad


def solution(mesh):
    in_specs = (P("col", "row"), P("row", "col"), P("row", "col"))
    out_specs = (P("row", "col"), P("col", "row"), P("row", "col"))
    return jax.shard_map(body, mesh=mesh, in_specs=in_specs, out_specs=out_specs, check_vma=False)
```

```python
import jax
import jax.numpy as jnp
from jax import lax
from jax.experimental.layout import Layout, with_layout_constraint
from jax.sharding import PartitionSpec as P

NX, NY, NZ, NC = 4, 4, 8, 2
BOTH = ("row", "col")


def activate(value):
    return jax.nn.gelu(value, approximate=True)


def pairs(step):
    out = []
    for x in range(NX):
        for y in range(NY):
            for z in range(NZ):
                for c in range(NC):
                    tx, ty, tz, tc = step(x, y, z, c)
                    source = ((x * NY + y) * NZ + z) * NC + c
                    target = (((tx % NX) * NY + ty % NY) * NZ + tz % NZ) * NC + tc % NC
                    out.append((source, target))
    return out


def way(c):
    return 1 - 2 * c


def along(first):
    return lambda d: pairs(
        lambda x, y, z, c: (x + d, y, z, c) if (c == 0) == first else (x, y + d, z, c)
    )


MOVES = {
    "first": along(True),
    "second": along(False),
    "z": lambda d: pairs(lambda x, y, z, c: (x, y, z + d * way(c), c)),
}
SWAP = pairs(lambda x, y, z, c: (x, y, z, 1 - c))


def send(value, axis, ahead):
    return lax.ppermute(value, BOTH, MOVES[axis](ahead))


def swap(value):
    return lax.ppermute(value, BOTH, SWAP)


def plainly(value):
    return with_layout_constraint(value, Layout(major_to_minor=tuple(range(value.ndim))))


def together(*values):
    return lax.optimization_barrier(values)


def reduce4(term, axis):
    bf16, f32 = jnp.bfloat16, jnp.float32
    out = together(*[plainly(term(m, h).astype(bf16)) for m, h in ((2, 0), (2, 1), (1, 1), (3, 0))])
    far_up, far_down = send(out[0], axis, 1), send(out[1], axis, -1)
    direct = [send(out[3], axis, -1), send(out[2], axis, 1)]
    relayed = [
        send((term(1, 0) + far_up.astype(f32)).astype(bf16), axis, 1),
        send((term(3, 1) + far_down.astype(f32)).astype(bf16), axis, -1),
    ]
    sums = [term(0, h) + direct[h].astype(f32) for h in range(2)]
    sums, relayed = together(sums, relayed)
    return [sums[h] + relayed[h].astype(f32) for h in range(2)]


def reduce4_direct(term, axis):
    bf16, f32 = jnp.bfloat16, jnp.float32
    out = together(*[plainly(term(m).astype(bf16)) for m in (2, 1, 3)])
    got = [send(part, axis, m) for part, m in zip(out, (2, 1, 3))]
    return sum((part.astype(f32) for part in got), term(0))


def gather4_direct(block, axis):
    block = plainly(block)
    got = {m: send(block, axis, -m) for m in (2, 1, 3)}
    return [block, got[1], got[2], got[3]]


def gather4(halves, axis):
    halves = [plainly(half) for half in halves]
    down = [send(halves[0], axis, 1), None]
    up = [None, send(halves[1], axis, -1)]
    down[1] = send(halves[1], axis, 1)
    up[0] = send(halves[0], axis, -1)
    far = [send(down[0], axis, 1), send(up[1], axis, -1)]
    return [halves, up, far, down]


def body(inputs, weight, out_grad):
    bf16, f32 = jnp.bfloat16, jnp.float32
    row, col = lax.axis_index("row"), lax.axis_index("col")
    x, y = row >> 2, row & 3
    z, core = col >> 1, col & 1
    up = way(core)
    tokens, features = inputs.shape
    hidden = weight.shape[1]

    def place(dz, other):
        at_z = (z + dz * up) & 7
        at_x, at_y = at_z >> 1, (at_z & 1) * 2 + ((core + other) & 1)
        return jnp.where(core == 0, ((at_x - x) & 3) * 4 + at_y, ((at_y - y) & 3) * 4 + at_x)

    with jax.named_scope("gather_inputs"):
        blocks = {(0, 0): inputs, (0, 1): swap(inputs)}
        pair = jnp.stack([blocks[0, 0], blocks[0, 1]])
        one = send(pair, "z", 1)
        two = send(pair, "z", 2)
        one, two = together(one, two)
        three = send(two, "z", 1)
        four = send(two[0], "z", 2)
        one, two, three, four = together(one, two, three, four)
        crossed = [swap(block) for block in (one, two, three, four)]
        for other in (0, 1):
            blocks[-1, other] = one[other]
            blocks[-2, other] = two[other]
            blocks[-3, other] = three[other]
            for dz in (1, 2, 3):
                blocks[dz, 1 - other] = crossed[dz - 1][other]
        blocks[4, 0] = four
        blocks[4, 1] = crossed[3]
        whole = jnp.zeros((16, tokens, features), bf16)
        for (dz, other), block in blocks.items():
            whole = lax.dynamic_update_index_in_dim(whole, block, place(dz, other), 0)
        whole = plainly(whole)

    def chunk(start, stop):
        return whole[start:stop].reshape((stop - start) * tokens, features)

    second = jnp.where(core == 0, y, x)
    with jax.named_scope("reduce_preact"):

        def part(m, h):
            start = 4 * m + 2 * h
            return jnp.dot(chunk(start, start + 2), weight, preferred_element_type=f32)

        total = jnp.concatenate(reduce4(part, "first")).reshape(4, tokens, hidden)

        def piece(m):
            return lax.dynamic_index_in_dim(total, (second + m) & 3, 0, keepdims=False)

        preact = reduce4_direct(piece, "second")
    with jax.named_scope("gelu"):
        activated, pullback = jax.vjp(activate, preact)
        activated = activated.astype(bf16)
        grad = pullback(out_grad.astype(f32))[0].astype(bf16)
        activated, grad = together(activated, grad)

    def to_inputs(block):
        return lax.dot_general(block, weight, (((1,), (1,)), ((), ())), preferred_element_type=f32)

    def to_weight(start, stop, block):
        return lax.dot_general(
            chunk(start, stop), block, (((0,), (0,)), ((), ())), preferred_element_type=f32
        )

    with jax.named_scope("gather_grad"):
        wide = jnp.zeros((4, tokens, hidden), bf16)
        for m, block in enumerate(gather4_direct(grad, "second")):
            wide = lax.dynamic_update_index_in_dim(wide, block, (second + m) & 3, 0)
        got = gather4([wide[:2].reshape(2 * tokens, hidden), wide[2:].reshape(2 * tokens, hidden)], "first")
        total = jnp.concatenate([to_inputs(got[m][h]) for m in range(4) for h in range(2)])

    with jax.named_scope("reduce_input_grad"):
        total = total.reshape(16, tokens, features)

        def pick(dz, other):
            return lax.dynamic_index_in_dim(total, place(dz, other), 0, keepdims=False)

        order = [(4, 0), (0, 0), (3, 0), (3, 1), (1, 0), (1, 1), (2, 0), (2, 1)]
        mine = jnp.stack([pick(dz, other) for dz, other in order])
        yours = jnp.stack([pick(-dz, 1 - other) for dz, other in order])
        kept, got = together(mine + swap(yours.astype(bf16)).astype(f32), got)
        near = send(kept[2:6].astype(bf16), "z", 1)
        four = send(kept[0].astype(bf16), "z", 2)
        pieces = [(m, h) for m in (0, 1, 3, 2) for h in range(2)]

        def weight_part(some):
            return sum(to_weight(4 * m + 2 * h, 4 * m + 2 * h + 2, got[m][h]) for m, h in some)

        four, got = together(four, got)
        early = weight_part(pieces[:4])
        near, early, got = together(near, early, got)
        two = kept[6:8] + near[:2].astype(f32)
        two = two.at[0].add(four.astype(f32)).astype(bf16)
        late = weight_part(pieces[4:])
        two, weight_grad = together(send(two, "z", 2), (early + late).astype(bf16))
        here = two.astype(f32) + near[2:].astype(f32)
        input_grad = kept[1] + here[0] + swap(here[1])
    return activated, input_grad.astype(bf16), weight_grad


def solution(mesh):
    in_specs = (P("col", "row"), P("row", "col"), P("row", "col"))
    out_specs = (P("row", "col"), P("col", "row"), P("row", "col"))
    return jax.shard_map(body, mesh=mesh, in_specs=in_specs, out_specs=out_specs, check_vma=False)
```

```python
import jax
import jax.numpy as jnp
from jax import lax
from jax.experimental.layout import Layout, with_layout_constraint
from jax.sharding import PartitionSpec as P

NX, NY, NZ, NC = 4, 4, 8, 2
BOTH = ("row", "col")


def activate(value):
    return jax.nn.gelu(value, approximate=True)


def pairs(step):
    out = []
    for x in range(NX):
        for y in range(NY):
            for z in range(NZ):
                for c in range(NC):
                    tx, ty, tz, tc = step(x, y, z, c)
                    source = ((x * NY + y) * NZ + z) * NC + c
                    target = (((tx % NX) * NY + ty % NY) * NZ + tz % NZ) * NC + tc % NC
                    out.append((source, target))
    return out


def way(c):
    return 1 - 2 * c


def along(first):
    return lambda d: pairs(
        lambda x, y, z, c: (x + d, y, z, c) if (c == 0) == first else (x, y + d, z, c)
    )


MOVES = {
    "first": along(True),
    "second": along(False),
    "z": lambda d: pairs(lambda x, y, z, c: (x, y, z + d * way(c), c)),
}
SWAP = pairs(lambda x, y, z, c: (x, y, z, 1 - c))


def send(value, axis, ahead):
    return lax.ppermute(value, BOTH, MOVES[axis](ahead))


def swap(value):
    return lax.ppermute(value, BOTH, SWAP)


def plainly(value):
    return with_layout_constraint(value, Layout(major_to_minor=tuple(range(value.ndim))))


def together(*values):
    return lax.optimization_barrier(values)


def reduce4(term, axis):
    bf16, f32 = jnp.bfloat16, jnp.float32
    out = together(*[plainly(term(m, h).astype(bf16)) for m, h in ((2, 0), (2, 1), (1, 1), (3, 0))])
    far_up, far_down = send(out[0], axis, 1), send(out[1], axis, -1)
    direct = [send(out[3], axis, -1), send(out[2], axis, 1)]
    relayed = [
        send((term(1, 0) + far_up.astype(f32)).astype(bf16), axis, 1),
        send((term(3, 1) + far_down.astype(f32)).astype(bf16), axis, -1),
    ]
    sums = [term(0, h) + direct[h].astype(f32) for h in range(2)]
    sums, relayed = together(sums, relayed)
    return [sums[h] + relayed[h].astype(f32) for h in range(2)]


def reduce4_direct(term, axis):
    bf16, f32 = jnp.bfloat16, jnp.float32
    out = together(*[plainly(term(m).astype(bf16)) for m in (2, 1, 3)])
    got = [send(part, axis, m) for part, m in zip(out, (2, 1, 3))]
    return sum((part.astype(f32) for part in got), term(0))


def gather4_direct(block, axis):
    block = plainly(block)
    got = {m: send(block, axis, -m) for m in (2, 1, 3)}
    return [block, got[1], got[2], got[3]]


def gather4(halves, axis):
    halves = [plainly(half) for half in halves]
    down = [send(halves[0], axis, 1), None]
    up = [None, send(halves[1], axis, -1)]
    down[1] = send(halves[1], axis, 1)
    up[0] = send(halves[0], axis, -1)
    far = [send(down[0], axis, 1), send(up[1], axis, -1)]
    return [halves, up, far, down]


def body(inputs, weight, out_grad):
    bf16, f32 = jnp.bfloat16, jnp.float32
    row, col = lax.axis_index("row"), lax.axis_index("col")
    x, y = row >> 2, row & 3
    z, core = col >> 1, col & 1
    up = way(core)
    start = row >> 4
    tokens, features = inputs.shape
    hidden = weight.shape[1]

    def place(dz, other):
        at_z = (z + dz * up) & 7
        at_x, at_y = at_z >> 1, (at_z & 1) * 2 + ((core + other) & 1)
        up_x, up_y = (at_x - x) & 3, (at_y - y) & 3
        return jnp.where(core == 0, up_x * 4 + up_y, up_y * 4 + up_x)

    with jax.named_scope("gather_inputs"):
        blocks = {(0, 0): inputs, (0, 1): swap(inputs)}
        pair = jnp.zeros((2, tokens, features), bf16)
        for other in (0, 1):
            pair = lax.dynamic_update_index_in_dim(pair, blocks[0, other], start + other, 0)
        one = send(pair, "z", 1)
        two = send(pair, "z", 2)
        one, two = together(one, two)
        three = send(two, "z", 1)
        four = send(two[0], "z", 2)
        one, two, three, four = together(one, two, three, four)
        crossed = [swap(block) for block in (one, two, three, four)]
        for other in (0, 1):
            blocks[-1, other] = one[other]
            blocks[-2, other] = two[other]
            blocks[-3, other] = three[other]
            for dz in (1, 2, 3):
                blocks[dz, 1 - other] = crossed[dz - 1][other]
        blocks[4, 0] = four
        blocks[4, 1] = crossed[3]
        whole = jnp.zeros((16, tokens, features), bf16)
        for (dz, other), block in blocks.items():
            whole = lax.dynamic_update_index_in_dim(whole, block, place(dz, other), 0)
        whole = plainly(whole)

    def chunk(start, stop):
        return whole[start:stop].reshape((stop - start) * tokens, features)

    with jax.named_scope("reduce_preact"):

        def part(m, h):
            block = 4 * m + 2 * h
            return jnp.dot(chunk(block, block + 2), weight, preferred_element_type=f32)

        totals = reduce4(part, "first")
        preact = reduce4_direct(
            lambda m: totals[m // 2].reshape(2, tokens, hidden)[m % 2], "second"
        )
    with jax.named_scope("gelu"):
        activated, pullback = jax.vjp(activate, preact)
        activated = activated.astype(bf16)
        grad = pullback(out_grad.astype(f32))[0].astype(bf16)
        activated, grad = together(activated, grad)

    def to_inputs(block):
        return lax.dot_general(block, weight, (((1,), (1,)), ((), ())), preferred_element_type=f32)

    def to_weight(start, stop, block):
        return lax.dot_general(
            chunk(start, stop), block, (((0,), (0,)), ((), ())), preferred_element_type=f32
        )

    with jax.named_scope("gather_grad"):
        wide = jnp.zeros((4, tokens, hidden), bf16)
        for m, block in enumerate(gather4_direct(grad, "second")):
            wide = lax.dynamic_update_index_in_dim(wide, block, start + m, 0)
        got = gather4([wide[:2].reshape(2 * tokens, hidden), wide[2:].reshape(2 * tokens, hidden)], "first")
        total = jnp.concatenate([to_inputs(got[m][h]) for m in range(4) for h in range(2)])

    with jax.named_scope("reduce_input_grad"):
        total = total.reshape(16, tokens, features)

        def pick(dz, other):
            return lax.dynamic_index_in_dim(total, place(dz, other), 0, keepdims=False)

        order = [(4, 0), (0, 0), (3, 0), (3, 1), (1, 0), (1, 1), (2, 0), (2, 1)]
        mine = jnp.stack([pick(dz, other) for dz, other in order])
        yours = jnp.stack([pick(-dz, 1 - other) for dz, other in order])
        kept, got = together(mine + swap(yours.astype(bf16)).astype(f32), got)
        near = send(kept[2:6].astype(bf16), "z", 1)
        four = send(kept[0].astype(bf16), "z", 2)
        pieces = [(m, h) for m in (0, 1, 3, 2) for h in range(2)]

        def weight_part(some):
            return sum(to_weight(4 * m + 2 * h, 4 * m + 2 * h + 2, got[m][h]) for m, h in some)

        four, got = together(four, got)
        early = weight_part(pieces[:4])
        near, early, got = together(near, early, got)
        two = kept[6:8] + near[:2].astype(f32)
        two = two.at[0].add(four.astype(f32)).astype(bf16)
        late = weight_part(pieces[4:])
        two, weight_grad = together(send(two, "z", 2), (early + late).astype(bf16))
        here = two.astype(f32) + near[2:].astype(f32)
        input_grad = kept[1] + here[0] + swap(here[1])
    return activated, input_grad.astype(bf16), weight_grad


def solution(mesh):
    in_specs = (P("col", "row"), P("row", "col"), P("row", "col"))
    out_specs = (P("row", "col"), P("col", "row"), P("row", "col"))
    return jax.shard_map(body, mesh=mesh, in_specs=in_specs, out_specs=out_specs, check_vma=False)
```

```python
import jax
import jax.numpy as jnp
from jax import lax
from jax.experimental.layout import Layout, with_layout_constraint
from jax.sharding import PartitionSpec as P

NX, NY, NZ, NC = 4, 4, 8, 2
BOTH = ("row", "col")


def activate(value):
    return jax.nn.gelu(value, approximate=True)


def pairs(step):
    out = []
    for x in range(NX):
        for y in range(NY):
            for z in range(NZ):
                for c in range(NC):
                    tx, ty, tz, tc = step(x, y, z, c)
                    source = ((x * NY + y) * NZ + z) * NC + c
                    target = (((tx % NX) * NY + ty % NY) * NZ + tz % NZ) * NC + tc % NC
                    out.append((source, target))
    return out


def way(c):
    return 1 - 2 * c


def along(first):
    return lambda d: pairs(
        lambda x, y, z, c: (x + d, y, z, c) if (c == 0) == first else (x, y + d, z, c)
    )


MOVES = {
    "first": along(True),
    "second": along(False),
    "z": lambda d: pairs(lambda x, y, z, c: (x, y, z + d * way(c), c)),
}
SWAP = pairs(lambda x, y, z, c: (x, y, z, 1 - c))


def send(value, axis, ahead):
    return lax.ppermute(value, BOTH, MOVES[axis](ahead))


def swap(value):
    return lax.ppermute(value, BOTH, SWAP)


def plainly(value):
    return with_layout_constraint(value, Layout(major_to_minor=tuple(range(value.ndim))))


def together(*values):
    return lax.optimization_barrier(values)


def reduce4(term, axis):
    bf16, f32 = jnp.bfloat16, jnp.float32
    out = together(*[plainly(term(m, h).astype(bf16)) for m, h in ((2, 0), (2, 1), (1, 1), (3, 0))])
    far_up, far_down = send(out[0], axis, 1), send(out[1], axis, -1)
    direct = [send(out[3], axis, -1), send(out[2], axis, 1)]
    relayed = [
        send((term(1, 0) + far_up.astype(f32)).astype(bf16), axis, 1),
        send((term(3, 1) + far_down.astype(f32)).astype(bf16), axis, -1),
    ]
    sums = [term(0, h) + direct[h].astype(f32) for h in range(2)]
    sums, relayed = together(sums, relayed)
    return [sums[h] + relayed[h].astype(f32) for h in range(2)]


def reduce4_direct(term, values, axis):
    bf16, f32 = jnp.bfloat16, jnp.float32
    out = together(*[plainly(term(values, m).astype(bf16)) for m in (2, 1, 3)])
    got = [send(part, axis, m) for part, m in zip(out, (2, 1, 3))]
    got, values = together(got, values)
    return sum((part.astype(f32) for part in got), term(values, 0))


def gather4_direct(block, axis):
    block = plainly(block)
    got = {m: send(block, axis, -m) for m in (2, 1, 3)}
    return [block, got[1], got[2], got[3]]


def gather4(halves, axis):
    halves = [plainly(half) for half in halves]
    down = [send(halves[0], axis, 1), None]
    up = [None, send(halves[1], axis, -1)]
    down[1] = send(halves[1], axis, 1)
    up[0] = send(halves[0], axis, -1)
    far = [send(down[0], axis, 1), send(up[1], axis, -1)]
    return [halves, up, far, down]


def body(inputs, weight, out_grad):
    bf16, f32 = jnp.bfloat16, jnp.float32
    row, col = lax.axis_index("row"), lax.axis_index("col")
    x, y = row >> 2, row & 3
    z, core = col >> 1, col & 1
    up = way(core)
    start = row >> 4
    tokens, features = inputs.shape
    hidden = weight.shape[1]

    def place(dz, other):
        at_z = (z + dz * up) & 7
        at_x, at_y = at_z >> 1, (at_z & 1) * 2 + ((core + other) & 1)
        up_x, up_y = (at_x - x) & 3, (at_y - y) & 3
        return jnp.where(core == 0, up_x * 4 + up_y, up_y * 4 + up_x)

    with jax.named_scope("gather_inputs"):
        blocks = {(0, 0): inputs, (0, 1): swap(inputs)}
        pair = jnp.zeros((2, tokens, features), bf16)
        for other in (0, 1):
            pair = lax.dynamic_update_index_in_dim(pair, blocks[0, other], start + other, 0)
        one = send(pair, "z", 1)
        two = send(pair, "z", 2)
        one, two = together(one, two)
        three = send(two, "z", 1)
        four = send(two[0], "z", 2)
        one, two, three, four = together(one, two, three, four)
        crossed = [swap(block) for block in (one, two, three, four)]
        for other in (0, 1):
            blocks[-1, other] = one[other]
            blocks[-2, other] = two[other]
            blocks[-3, other] = three[other]
            for dz in (1, 2, 3):
                blocks[dz, 1 - other] = crossed[dz - 1][other]
        blocks[4, 0] = four
        blocks[4, 1] = crossed[3]
        whole = jnp.zeros((16, tokens, features), bf16)
        for (dz, other), block in blocks.items():
            whole = lax.dynamic_update_index_in_dim(whole, block, place(dz, other), 0)
        whole = plainly(whole)

    def chunk(start, stop):
        return whole[start:stop].reshape((stop - start) * tokens, features)

    with jax.named_scope("reduce_preact"):

        def part(m, h):
            block = 4 * m + 2 * h
            return jnp.dot(chunk(block, block + 2), weight, preferred_element_type=f32)

        totals = reduce4(part, "first")
        preact = reduce4_direct(
            lambda halves, m: halves[m // 2].reshape(2, tokens, hidden)[m % 2], totals, "second"
        )
    with jax.named_scope("gelu"):
        activated, pullback = jax.vjp(activate, preact)
        activated = activated.astype(bf16)
        grad = pullback(out_grad.astype(f32))[0].astype(bf16)
        activated, grad = together(activated, grad)

    def to_inputs(block):
        return lax.dot_general(block, weight, (((1,), (1,)), ((), ())), preferred_element_type=f32)

    def to_weight(start, stop, block):
        return lax.dot_general(
            chunk(start, stop), block, (((0,), (0,)), ((), ())), preferred_element_type=f32
        )

    with jax.named_scope("gather_grad"):
        wide = jnp.zeros((4, tokens, hidden), bf16)
        for m, block in enumerate(gather4_direct(grad, "second")):
            wide = lax.dynamic_update_index_in_dim(wide, block, start + m, 0)
        got = gather4([wide[:2].reshape(2 * tokens, hidden), wide[2:].reshape(2 * tokens, hidden)], "first")
        total = jnp.zeros((16 * tokens, features), f32)

        def add_inputs(total, m):
            for h in range(2):
                total = lax.dynamic_update_slice(total, to_inputs(got[m][h]), ((4 * m + 2 * h) * tokens, 0))
            return total

        for m in (0, 1, 3):
            total = add_inputs(total, m)
        total, got[2] = together(total, got[2])
        total = add_inputs(total, 2)

    with jax.named_scope("reduce_input_grad"):
        total = total.reshape(16, tokens, features)

        def pick(dz, other):
            return lax.dynamic_index_in_dim(total, place(dz, other), 0, keepdims=False)

        order = [(4, 0), (0, 0), (3, 0), (3, 1), (1, 0), (1, 1), (2, 0), (2, 1)]
        mine = jnp.stack([pick(dz, other) for dz, other in order])
        yours = jnp.stack([pick(-dz, 1 - other) for dz, other in order])
        kept, got = together(mine + swap(yours.astype(bf16)).astype(f32), got)
        near = send(kept[2:6].astype(bf16), "z", 1)
        four = send(kept[0].astype(bf16), "z", 2)
        pieces = [(m, h) for m in (0, 1, 3, 2) for h in range(2)]

        def weight_part(some):
            return sum(to_weight(4 * m + 2 * h, 4 * m + 2 * h + 2, got[m][h]) for m, h in some)

        four, got = together(four, got)
        early = weight_part(pieces[:4])
        near, early, got = together(near, early, got)
        two = kept[6:8] + near[:2].astype(f32)
        two = two.at[0].add(four.astype(f32)).astype(bf16)
        late = weight_part(pieces[4:])
        two, weight_grad = together(send(two, "z", 2), (early + late).astype(bf16))
        here = two.astype(f32) + near[2:].astype(f32)
        input_grad = kept[1] + here[0] + swap(here[1])
    return activated, input_grad.astype(bf16), weight_grad


def solution(mesh):
    in_specs = (P("col", "row"), P("row", "col"), P("row", "col"))
    out_specs = (P("row", "col"), P("col", "row"), P("row", "col"))
    return jax.shard_map(body, mesh=mesh, in_specs=in_specs, out_specs=out_specs, check_vma=False)
```

```python
import jax
import jax.numpy as jnp
from jax import lax
from jax.experimental.layout import Layout, with_layout_constraint
from jax.sharding import PartitionSpec as P

NX, NY, NZ, NC = 4, 4, 8, 2
BOTH = ("row", "col")


def activate(value):
    return jax.nn.gelu(value, approximate=True)


def pairs(step):
    out = []
    for x in range(NX):
        for y in range(NY):
            for z in range(NZ):
                for c in range(NC):
                    tx, ty, tz, tc = step(x, y, z, c)
                    source = ((x * NY + y) * NZ + z) * NC + c
                    target = (((tx % NX) * NY + ty % NY) * NZ + tz % NZ) * NC + tc % NC
                    out.append((source, target))
    return out


def way(c):
    return 1 - 2 * c


def along(first):
    return lambda d: pairs(
        lambda x, y, z, c: (x + d, y, z, c) if (c == 0) == first else (x, y + d, z, c)
    )


MOVES = {
    "first": along(True),
    "second": along(False),
    "z": lambda d: pairs(lambda x, y, z, c: (x, y, z + d * way(c), c)),
}
SWAP = pairs(lambda x, y, z, c: (x, y, z, 1 - c))


def send(value, axis, ahead):
    return lax.ppermute(value, BOTH, MOVES[axis](ahead))


def swap(value):
    return lax.ppermute(value, BOTH, SWAP)


def plainly(value):
    return with_layout_constraint(value, Layout(major_to_minor=tuple(range(value.ndim))))


def together(*values):
    return lax.optimization_barrier(values)


def reduce4(term, axis):
    bf16, f32 = jnp.bfloat16, jnp.float32
    out = [plainly(term(m, h).astype(bf16)) for m, h in ((2, 0), (2, 1), (1, 1), (3, 0))]
    out = [*together(*out[:2]), *together(*out[2:])]
    far_up, far_down = send(out[0], axis, 1), send(out[1], axis, -1)
    direct = [send(out[3], axis, -1), send(out[2], axis, 1)]
    relayed = [
        send((term(1, 0) + far_up.astype(f32)).astype(bf16), axis, 1),
        send((term(3, 1) + far_down.astype(f32)).astype(bf16), axis, -1),
    ]
    sums = [term(0, h) + direct[h].astype(f32) for h in range(2)]
    sums, relayed = together(sums, relayed)
    return sums, relayed


def reduce4_direct(term, values, axis):
    bf16, f32 = jnp.bfloat16, jnp.float32
    out = together(*[plainly(term(values, m).astype(bf16)) for m in (2, 1, 3)])
    got = [send(part, axis, m) for part, m in zip(out, (2, 1, 3))]
    got, values = together(got, values)
    return sum((part.astype(f32) for part in got), term(values, 0))


def gather4_direct(block, axis):
    block = plainly(block)
    got = {m: send(block, axis, -m) for m in (2, 1, 3)}
    return [block, got[1], got[2], got[3]]


def gather4(halves, axis):
    halves = [plainly(half) for half in halves]
    down = [send(halves[0], axis, 1), None]
    up = [None, send(halves[1], axis, -1)]
    down[1] = send(halves[1], axis, 1)
    up[0] = send(halves[0], axis, -1)
    far = [send(down[0], axis, 1), send(up[1], axis, -1)]
    return [halves, up, far, down]


def body(inputs, weight, out_grad):
    bf16, f32 = jnp.bfloat16, jnp.float32
    row, col = lax.axis_index("row"), lax.axis_index("col")
    x, y = row >> 2, row & 3
    z, core = col >> 1, col & 1
    up = way(core)
    start = row >> 4
    tokens, features = inputs.shape
    hidden = weight.shape[1]

    def place(dz, other):
        at_z = (z + dz * up) & 7
        at_x, at_y = at_z >> 1, (at_z & 1) * 2 + ((core + other) & 1)
        up_x, up_y = (at_x - x) & 3, (at_y - y) & 3
        return jnp.where(core == 0, up_x * 4 + up_y, up_y * 4 + up_x)

    with jax.named_scope("gather_inputs"):
        blocks = {(0, 0): inputs, (0, 1): swap(inputs)}
        pair = jnp.zeros((2, tokens, features), bf16)
        for other in (0, 1):
            pair = lax.dynamic_update_index_in_dim(pair, blocks[0, other], start + other, 0)
        one = send(pair, "z", 1)
        two = send(pair, "z", 2)
        one, two = together(one, two)
        three = send(two, "z", 1)
        four = send(two[0], "z", 2)
        one, two, three, four = together(one, two, three, four)
        crossed = [swap(block) for block in (one, two, three, four)]
        for other in (0, 1):
            blocks[-1, other] = one[other]
            blocks[-2, other] = two[other]
            blocks[-3, other] = three[other]
            for dz in (1, 2, 3):
                blocks[dz, 1 - other] = crossed[dz - 1][other]
        blocks[4, 0] = four
        blocks[4, 1] = crossed[3]
        whole = jnp.zeros((16, tokens, features), bf16)
        for (dz, other), block in blocks.items():
            whole = lax.dynamic_update_index_in_dim(whole, block, place(dz, other), 0)
        whole = plainly(whole)

    def chunk(start, stop):
        return whole[start:stop].reshape((stop - start) * tokens, features)

    with jax.named_scope("reduce_preact"):

        def part(m, h):
            block = 4 * m + 2 * h
            return jnp.dot(chunk(block, block + 2), weight, preferred_element_type=f32)

        totals = reduce4(part, "first")
        preact = reduce4_direct(
            lambda two, m: sum(
                halves[m // 2].reshape(2, tokens, hidden)[m % 2].astype(f32) for halves in two
            ),
            totals,
            "second",
        )
    with jax.named_scope("gelu"):
        activated, pullback = jax.vjp(activate, preact)
        activated = activated.astype(bf16)
        grad = pullback(out_grad.astype(f32))[0].astype(bf16)
        activated, grad = together(activated, grad)

    def to_inputs(block):
        return lax.dot_general(block, weight, (((1,), (1,)), ((), ())), preferred_element_type=f32)

    def to_weight(start, stop, block):
        return lax.dot_general(
            chunk(start, stop), block, (((0,), (0,)), ((), ())), preferred_element_type=f32
        )

    with jax.named_scope("gather_grad"):
        wide = jnp.zeros((4, tokens, hidden), bf16)
        for m, block in enumerate(gather4_direct(grad, "second")):
            wide = lax.dynamic_update_index_in_dim(wide, block, start + m, 0)
        got = gather4([wide[:2].reshape(2 * tokens, hidden), wide[2:].reshape(2 * tokens, hidden)], "first")
        total = jnp.zeros((16 * tokens, features), f32)

        def add_inputs(total, m):
            for h in range(2):
                total = lax.dynamic_update_slice(total, to_inputs(got[m][h]), ((4 * m + 2 * h) * tokens, 0))
            return total

        for m in (0, 1, 3):
            total = add_inputs(total, m)
        total, got[2] = together(total, got[2])
        total = add_inputs(total, 2)

    with jax.named_scope("reduce_input_grad"):
        total = total.reshape(16, tokens, features)

        def pick(dz, other):
            return lax.dynamic_index_in_dim(total, place(dz, other), 0, keepdims=False)

        order = [(4, 0), (0, 0), (3, 0), (3, 1), (1, 0), (1, 1), (2, 0), (2, 1)]
        mine = jnp.stack([pick(dz, other) for dz, other in order])
        yours = jnp.stack([pick(-dz, 1 - other) for dz, other in order])
        kept, got = together(mine + swap(yours.astype(bf16)).astype(f32), got)
        near = send(kept[2:6].astype(bf16), "z", 1)
        four = send(kept[0].astype(bf16), "z", 2)
        pieces = [(m, h) for m in (0, 1, 3, 2) for h in range(2)]

        def weight_part(some):
            return sum(to_weight(4 * m + 2 * h, 4 * m + 2 * h + 2, got[m][h]) for m, h in some)

        four, got = together(four, got)
        early = weight_part(pieces[:4])
        near, early, got = together(near, early, got)
        two = kept[6:8] + near[:2].astype(f32)
        two = two.at[0].add(four.astype(f32)).astype(bf16)
        late = weight_part(pieces[4:])
        two, weight_grad = together(send(two, "z", 2), (early + late).astype(bf16))
        here = two.astype(f32) + near[2:].astype(f32)
        input_grad = kept[1] + here[0] + swap(here[1])
    return activated, input_grad.astype(bf16), weight_grad


def solution(mesh):
    in_specs = (P("col", "row"), P("row", "col"), P("row", "col"))
    out_specs = (P("row", "col"), P("col", "row"), P("row", "col"))
    return jax.shard_map(body, mesh=mesh, in_specs=in_specs, out_specs=out_specs, check_vma=False)
```
